32 devices in a mesh: ctx: 8 (over y, x, core), tp: 4 (over z).
Axes of the slice: x: 2, y: 2, z: 4, core: 2. Of those that a mesh axis runs over, the one named last changes fastest.
Arguments:
- features: bfloat16 [2048, 3, 4096], P('ctx', None, 'tp'), may hold values from -6 to 6
- short_taps: float32 [3, 3, 4096], P(None, None, 'tp'), may hold values from -3.5 to 3.5
- residues: float32 [16, 256], P(None, 'tp'), may hold values from -1.5 to 1.5
- rates: float32 [16, 256], P(None, 'tp'), may hold values from 0.000146484375 to 0.05, as said below
- skip: float32 [4096], P('tp'), may hold values from -4 to 4
- out_weight: bfloat16 [4096, 4096], P(None, 'tp'), may hold values from -0.09375 to 0.09375
Outputs:
- mixed: bfloat16 [2048, 4096], P('ctx', 'tp')
The draws below stay inside these ranges and needn't reach their ends.
Inputs may be any that keep to these rules, and one draw needn't show every extreme that they name: `rates`: decay rate of one mode of one filter.
All inputs are finite; a program needn't handle non-finite values.
Results may differ from the reference program's by a relative error of at most 0.0049.
Values may be sent and summed in bfloat16 or wider, within the bound.
A program may use at most 128 MiB of HBM per device.

```python
import jax
import jax.numpy as jnp
from jax import lax

D = 4096
GROUP = 16
ORDER = 16
SHORT = 3
SEQ = 2048
FILTERS = 256


def draw_rates(key, part):
    uniform_part = jax.random.uniform(key, (ORDER, FILTERS), jnp.float32)
    lowest = 0.3 / SEQ
    highest = 0.05
    return jnp.exp(jnp.log(lowest) + uniform_part * (jnp.log(highest) - jnp.log(lowest)))


def steps_of(own_key, dims, shards, low, largest):
    level, own = 1.0, jax.random.fold_in(own_key, 6)
    for dim, shards_of in shards:
        steps = jnp.exp(jax.random.uniform(jax.random.fold_in(own, dim), (shards_of,), jnp.float32, low / len(shards), largest / len(shards)))
        level = level * jnp.repeat(steps, dims[dim] // shards_of).reshape([-1 if axis == dim else 1 for axis in range(len(dims))])
    return level


def scatter_about(stream_key, shape, scale, most, cuts=(), held_as=jnp.bfloat16):
    gain = steps_of(stream_key, shape, cuts, -0.22, 0.18) if cuts else 1.0
    array = jax.random.normal(stream_key, shape, jnp.float32) * scale * gain
    return jnp.minimum(jnp.maximum(array, -most), most).astype(held_as)


def setup_inputs(seed: int = 0) -> dict:
    seeds = jax.random.split(jax.random.key(seed), 7)
    features = scatter_about(seeds[0], (SEQ, 3, D), 1.0, 6.0, ((0, 8), (2, 4)))
    short_taps = scatter_about(seeds[1], (SHORT, 3, D), SHORT ** -0.5, 3.5, ((2, 4),), jnp.float32)
    residues = scatter_about(seeds[2], (ORDER, FILTERS), ORDER ** -0.5, 1.5, ((1, 4),), jnp.float32)
    rates = draw_rates(jax.random.fold_in(seeds[6], 71), 0)
    skip = scatter_about(seeds[4], (D,), 1.0, 4.0, ((0, 4),), jnp.float32)
    out_weight = scatter_about(seeds[5], (D, D), D ** -0.5, 0.09375, ((1, 4),))
    return dict(features=features, short_taps=short_taps, residues=residues, rates=rates, skip=skip, out_weight=out_weight)


column_block = 256

def short_filter(feats, taps):
    lead = jnp.zeros((SHORT - 1,) + feats.shape[1:], feats.dtype)
    extended = jnp.concatenate([lead, feats], 0)
    total = jnp.zeros(feats.shape, jnp.float32)
    for shift in range(SHORT):
        window = extended[SHORT - 1 - shift:SHORT - 1 - shift + SEQ].astype(jnp.float32)
        total = total + taps[shift] * window
    return total

def channel_block(pieces):
    feats, taps, skip_part, filt_part = pieces
    shorted = short_filter(feats, taps)
    query = shorted[:, 0, :]
    product = shorted[:, 1, :] * shorted[:, 2, :]
    spectrum = jnp.fft.rfft(product, n=2 * SEQ, axis=0) * jnp.fft.rfft(filt_part, n=2 * SEQ, axis=0)
    conv = jnp.fft.irfft(spectrum, n=2 * SEQ, axis=0)[:SEQ]
    return (query * (conv + skip_part * product)).astype(jnp.bfloat16)

def reference(features, short_taps, residues, rates, skip, out_weight):
    block_count = D // column_block
    positions = jnp.arange(SEQ).astype(jnp.float32)[:, None]
    filt = jnp.zeros((SEQ, FILTERS), jnp.float32)
    for order in range(ORDER):
        filt = filt + residues[order] * jnp.sqrt(2.0 * rates[order]) * jnp.exp(-rates[order] * positions)
    filt_full = jnp.repeat(filt, GROUP, axis=1)
    feats_blocks = features.reshape(SEQ, 3, block_count, column_block).transpose(2, 0, 1, 3)
    taps_blocks = short_taps.reshape(SHORT, 3, block_count, column_block).transpose(2, 0, 1, 3)
    skip_blocks = skip.reshape(block_count, column_block)
    filt_blocks = filt_full.reshape(SEQ, block_count, column_block).transpose(1, 0, 2)
    gated = lax.map(channel_block, (feats_blocks, taps_blocks, skip_blocks, filt_blocks))
    gated = gated.transpose(1, 0, 2).reshape(SEQ, D)
    return jnp.dot(gated, out_weight, preferred_element_type=jnp.float32).astype(jnp.bfloat16)
```

```python
import functools

import jax
import jax.numpy as jnp
from jax import lax
from jax.experimental import pallas as pl
from jax.experimental.pallas import tpu as pltpu
from jax.sharding import PartitionSpec as P

MESH = pl.DeviceIdType.MESH
LANES = 128
SPAN = 64
HALO = 16


def iota(shape, dim):
    return lax.broadcasted_iota(jnp.int32, shape, dim)


def split(x):
    high = x.astype(jnp.bfloat16)
    low = (x - high.astype(jnp.float32)).astype(jnp.bfloat16)
    return high, low


def dot(left, right, dims):
    return lax.dot_general(
        left, right, ((dims[:1], dims[1:]), ((), ())), preferred_element_type=jnp.float32
    )


def kernel(
    n_ctx, n_tp, group,
    feats, taps, residues, rates, skip, w_hbm, out,
    halo, w, gath, prod, query, conv, states, rep_rates, row_rates, row_coefs,
    entering, e_send, e_recv, acc,
    w_sem, halo_sems, es_sems, er_sems, left_sems, right_sems, fwd_sems, recv_sems,
):
    me, z = lax.axis_index("ctx"), lax.axis_index("tp")
    rows, width = feats.shape[1], feats.shape[2]
    modes, filters = rates.shape
    blocks, chunks = width // LANES, rows // SPAN
    per = LANES // group

    w_copy = pltpu.make_async_copy(w_hbm, w, w_sem)
    w_copy.start()

    barrier = pltpu.get_barrier_semaphore()

    def greet(d, _):
        pl.semaphore_signal(
            barrier, inc=1, device_id=(lax.rem(me + d, n_ctx), z), device_id_type=MESH
        )
        return 0

    lax.fori_loop(1, n_ctx, greet, 0)

    @pl.when(z > 0)
    def _():
        pl.semaphore_signal(barrier, inc=1, device_id=(me, z - 1), device_id_type=MESH)

    @pl.when(z < n_tp - 1)
    def _():
        pl.semaphore_signal(barrier, inc=1, device_id=(me, z + 1), device_id_type=MESH)

    pick = (iota((filters, width), 0) == iota((filters, width), 1) // group).astype(jnp.float32)

    def repeat(x):
        return lax.dot_general(
            x, pick, (((1,), (0,)), ((), ())),
            precision=lax.Precision.HIGHEST, preferred_element_type=jnp.float32,
        )

    diag = iota((modes, width), 0) == iota((modes, width), 1) % modes
    rep_rates[...] = repeat(rates[...])
    row_rates[...] = jnp.sum(jnp.where(diag, rep_rates[...], 0.0), axis=0, keepdims=True)
    row_res = jnp.sum(jnp.where(diag, repeat(residues[...]), 0.0), axis=0, keepdims=True)
    row_coefs[...] = row_res * jnp.sqrt(2.0 * row_rates[...])

    neighbours = (z > 0).astype(jnp.int32) + (z < n_tp - 1).astype(jnp.int32)
    pl.semaphore_wait(barrier, n_ctx - 1 + neighbours)

    halo_copy = pltpu.make_async_remote_copy(
        src_ref=feats.at[:, pl.ds(rows - HALO, HALO), :],
        dst_ref=halo,
        send_sem=halo_sems.at[0],
        recv_sem=halo_sems.at[1],
        device_id=(lax.rem(me + 1, n_ctx), z),
        device_id_type=MESH,
    )

    @pl.when(me < n_ctx - 1)
    def _():
        halo_copy.start()

    @pl.when(me == 0)
    def _():
        halo[...] = jnp.zeros_like(halo)

    @pl.when(me > 0)
    def _():
        halo_copy.wait_recv()

    def lanes_of(b):
        return pl.ds(pl.multiple_of(b * LANES, LANES), LANES)

    def wide(x):
        return jnp.concatenate([x[k * SPAN : (k + 1) * SPAN] for k in range(chunks)], axis=1)

    def shorted(b, j):
        lanes = lanes_of(b)
        here = feats[j, :, lanes].astype(jnp.float32)
        before = halo[j, :, lanes].astype(jnp.float32)
        row = iota((rows, LANES), 0)
        last, second = before[HALO - 1 : HALO], before[HALO - 2 : HALO - 1]
        one = jnp.where(row == 0, last, pltpu.roll(here, 1, 0))
        two = jnp.where(row == 0, second, jnp.where(row == 1, last, pltpu.roll(here, 2, 0)))
        tap = [taps[s, pl.ds(j, 1), lanes] for s in range(3)]
        return tap[0] * here + tap[1] * one + tap[2] * two

    def first(b, _):
        lanes = lanes_of(b)
        query[b] = shorted(b, 0)
        product = shorted(b, 1) * shorted(b, 2)
        prod[b] = product
        rate = row_rates[:, lanes]
        left_over = (SPAN - iota((SPAN, LANES), 0)).astype(jnp.float32)
        high, low = split(jnp.exp(-rate * left_over))
        value = wide(product).astype(jnp.bfloat16)
        full = dot(high, value, (0, 0)) + dot(low, value, (0, 0))
        own = iota(full.shape, 0) // modes == (iota(full.shape, 1) % LANES) // group
        full = jnp.where(own, full, 0.0)
        state = full[:modes]
        for f in range(1, per):
            state = state + full[f * modes : (f + 1) * modes]
        states[b] = state
        decay = jnp.exp(-float(SPAN) * rep_rates[:, lanes])
        total = state[:, :LANES]
        for k in range(1, chunks):
            total = total * decay + state[:, k * LANES : (k + 1) * LANES]
        e_send[:, lanes] = total.astype(jnp.bfloat16)
        return 0

    lax.fori_loop(0, blocks, first, 0)

    def e_copy(d):
        return pltpu.make_async_remote_copy(
            src_ref=e_send,
            dst_ref=e_recv.at[d - 1],
            send_sem=es_sems.at[d - 1],
            recv_sem=er_sems.at[d - 1],
            device_id=(lax.rem(me + d, n_ctx), z),
            device_id_type=MESH,
        )

    def e_start(d, _):
        @pl.when(me + d < n_ctx)
        def _():
            e_copy(d).start()

        return 0

    lax.fori_loop(1, n_ctx, e_start, 0)

    def within(b, _):
        lanes = lanes_of(b)
        rate, coef = row_rates[:, lanes], row_coefs[:, lanes]
        at = iota((SPAN, LANES), 0).astype(jnp.float32)
        a_high, a_low = split(coef * jnp.exp(-rate * at))
        rise = jnp.exp(rate * at)
        rise_high = rise.astype(jnp.bfloat16).astype(jnp.float32)
        rise_low = rise - rise_high
        shape = (per * SPAN, LANES)
        own = iota(shape, 0) // SPAN == iota(shape, 1) // modes
        b_high = jnp.where(own, jnp.concatenate([rise_high] * per, 0), 0.0).astype(jnp.bfloat16)
        b_low = jnp.where(own, jnp.concatenate([rise_low] * per, 0), 0.0).astype(jnp.bfloat16)
        filt = (
            dot(a_high, b_high, (1, 1)) + dot(a_low, b_high, (1, 1)) + dot(a_high, b_low, (1, 1))
        )
        filt = jnp.where(
            iota(filt.shape, 0) >= iota(filt.shape, 1) % SPAN, filt, 0.0
        ).astype(jnp.bfloat16)
        value = jnp.concatenate([wide(prod[b])] * per, 0)
        own = iota(value.shape, 0) // SPAN == (iota(value.shape, 1) % LANES) // group
        value = jnp.where(own, value, 0.0).astype(jnp.bfloat16)
        conv[b] = dot(filt, value, (1, 0))
        return 0

    lax.fori_loop(0, blocks, within, 0)

    entering[...] = jnp.zeros_like(entering)

    def e_take(d, _):
        @pl.when(me >= d)
        def _():
            e_copy(d).wait_recv()
            span = ((d - 1) * rows).astype(jnp.float32)
            entering[...] += jnp.exp(-span * rep_rates[...]) * e_recv[d - 1].astype(jnp.float32)

        return 0

    lax.fori_loop(1, n_ctx, e_take, 0)

    def own_copy(b, to, sems):
        return pltpu.make_async_remote_copy(
            src_ref=gath.at[z, b],
            dst_ref=gath.at[z, b],
            send_sem=sems.at[b],
            recv_sem=recv_sems.at[z, b],
            device_id=(me, to),
            device_id_type=MESH,
        )

    def finish(b, _):
        lanes = lanes_of(b)
        rate, coef = row_rates[:, lanes], row_coefs[:, lanes]
        at = iota((SPAN, LANES), 0).astype(jnp.float32)
        a_high, a_low = split(coef * jnp.exp(-rate * at))
        decay = jnp.exp(-float(SPAN) * rep_rates[:, lanes])
        held, parts, state = entering[:, lanes], [], states[b]
        for k in range(chunks):
            parts.append(held)
            held = held * decay + state[:, k * LANES : (k + 1) * LANES]
        tall = jnp.concatenate([jnp.concatenate(parts, axis=1)] * per, 0)
        own = iota(tall.shape, 0) // modes == (iota(tall.shape, 1) % LANES) // group
        tall = jnp.where(own, tall, 0.0).astype(jnp.bfloat16)
        total = conv[b] + dot(a_high, tall, (1, 0)) + dot(a_low, tall, (1, 0))
        direct = skip[:, lanes]
        for k in range(chunks):
            span = pl.ds(k * SPAN, SPAN)
            value = total[:, k * LANES : (k + 1) * LANES] + direct * prod[b, span, :]
            gath[z, b, span, :] = (query[b, span, :] * value).astype(jnp.bfloat16)

        @pl.when(z > 0)
        def _():
            own_copy(b, z - 1, left_sems).start()

        @pl.when(z < n_tp - 1)
        def _():
            own_copy(b, z + 1, right_sems).start()

        return 0

    lax.fori_loop(0, blocks, finish, 0)

    def project(shard, p):
        left = jnp.concatenate([gath[shard, 2 * p], gath[shard, 2 * p + 1]], axis=1)
        depth = 2 * LANES
        at = pl.multiple_of(shard * width + p * depth, depth)
        acc[...] += dot(left, w[pl.ds(at, depth), :], (1, 0))

    w_copy.wait()
    acc[...] = jnp.zeros_like(acc)

    def own_step(p, _):
        project(z, p)
        return 0

    lax.fori_loop(0, blocks // 2, own_step, 0)

    def pass_copy(shard, b, to):
        return pltpu.make_async_remote_copy(
            src_ref=gath.at[shard, b],
            dst_ref=gath.at[shard, b],
            send_sem=fwd_sems.at[shard, b],
            recv_sem=recv_sems.at[shard, b],
            device_id=(me, to),
            device_id_type=MESH,
        )

    def hop(i, _):
        d, p = 1 + i // (blocks // 2), i % (blocks // 2)
        above, below = z + d, z - d
        for b in (2 * p, 2 * p + 1):
            @pl.when(above < n_tp)
            def _():
                pass_copy(above, b, lax.rem(z + 1, n_tp)).wait_recv()

                @pl.when(z > 0)
                def _():
                    pass_copy(above, b, z - 1).start()

            @pl.when(below >= 0)
            def _():
                pass_copy(below, b, lax.rem(z + 1, n_tp)).wait_recv()

                @pl.when(z < n_tp - 1)
                def _():
                    pass_copy(below, b, z + 1).start()

        @pl.when(above < n_tp)
        def _():
            project(above, p)

        @pl.when(below >= 0)
        def _():
            project(below, p)

        return 0

    lax.fori_loop(0, (n_tp - 1) * (blocks // 2), hop, 0)
    out[...] = acc[...].astype(out.dtype)

    @pl.when(me < n_ctx - 1)
    def _():
        halo_copy.wait_send()

    def e_sent(d, _):
        @pl.when(me + d < n_ctx)
        def _():
            e_copy(d).wait_send()

        return 0

    lax.fori_loop(1, n_ctx, e_sent, 0)

    def own_sent(b, _):
        @pl.when(z > 0)
        def _():
            own_copy(b, z - 1, left_sems).wait_send()

        @pl.when(z < n_tp - 1)
        def _():
            own_copy(b, z + 1, right_sems).wait_send()

        return 0

    lax.fori_loop(0, blocks, own_sent, 0)

    def pass_sent(i, _):
        shard, b = i // blocks, i % blocks

        @pl.when((shard > z) & (z > 0))
        def _():
            pass_copy(shard, b, z - 1).wait_send()

        @pl.when((shard < z) & (z < n_tp - 1))
        def _():
            pass_copy(shard, b, z + 1).wait_send()

        return 0

    lax.fori_loop(0, n_tp * blocks, pass_sent, 0)


def shards(n_ctx, n_tp, features, short_taps, residues, rates, skip, out_weight):
    rows, _, width = features.shape
    modes, filters = rates.shape
    group = width // filters
    blocks, chunks = width // LANES, rows // SPAN
    columns = out_weight.shape[1]
    vmem = pl.BlockSpec(memory_space=pltpu.VMEM)
    f32, bf16 = jnp.float32, jnp.bfloat16
    dma = pltpu.SemaphoreType.DMA
    return pl.pallas_call(
        functools.partial(kernel, n_ctx, n_tp, group),
        out_shape=jax.ShapeDtypeStruct((rows, columns), bf16),
        in_specs=[vmem] * 5 + [pl.BlockSpec(memory_space=pl.ANY)],
        out_specs=vmem,
        scratch_shapes=[
            pltpu.VMEM((3, HALO, width), bf16),
            pltpu.VMEM(out_weight.shape, bf16),
            pltpu.VMEM((n_tp, blocks, rows, LANES), bf16),
            pltpu.VMEM((blocks, rows, LANES), f32),
            pltpu.VMEM((blocks, rows, LANES), f32),
            pltpu.VMEM((blocks, SPAN, chunks * LANES), f32),
            pltpu.VMEM((blocks, modes, chunks * LANES), f32),
            pltpu.VMEM((modes, width), f32),
            pltpu.VMEM((1, width), f32),
            pltpu.VMEM((1, width), f32),
            pltpu.VMEM((modes, width), f32),
            pltpu.VMEM((modes, width), bf16),
            pltpu.VMEM((n_ctx - 1, modes, width), bf16),
            pltpu.VMEM((rows, columns), f32),
            dma(()),
            dma((2,)),
            dma((n_ctx - 1,)),
            dma((n_ctx - 1,)),
            dma((blocks,)),
            dma((blocks,)),
            dma((n_tp, blocks)),
            dma((n_tp, blocks)),
        ],
        compiler_params=pltpu.CompilerParams(
            collective_id=0, has_side_effects=True, vmem_limit_bytes=48 * 1024 * 1024
        ),
        cost_estimate=pl.CostEstimate(
            flops=2 * rows * width * n_tp * columns,
            bytes_accessed=2 * out_weight.size,
            transcendentals=0,
        ),
    )(
        jnp.transpose(features, (1, 0, 2)), short_taps, residues, rates,
        skip.reshape(1, width), out_weight,
    )


def solution(mesh):
    in_specs = (
        P("ctx", None, "tp"),
        P(None, None, "tp"),
        P(None, "tp"),
        P(None, "tp"),
        P("tp"),
        P(None, "tp"),
    )
    n_ctx, n_tp = mesh.shape["ctx"], mesh.shape["tp"]
    return jax.shard_map(
        functools.partial(shards, n_ctx, n_tp),
        mesh=mesh, in_specs=in_specs, out_specs=P("ctx", "tp"), check_vma=False,
    )
```

```python
import functools

import jax
import jax.numpy as jnp
from jax import lax
from jax.experimental import pallas as pl
from jax.experimental.pallas import tpu as pltpu
from jax.sharding import PartitionSpec as P

MESH = pl.DeviceIdType.MESH
LANES = 128
SPAN = 64
AHEAD = 3
HALO = 16


def iota(shape, dim):
    return lax.broadcasted_iota(jnp.int32, shape, dim)


def split(x):
    high = x.astype(jnp.bfloat16)
    low = (x - high.astype(jnp.float32)).astype(jnp.bfloat16)
    return high, low


def dot(left, right, dims):
    return lax.dot_general(
        left, right, ((dims[:1], dims[1:]), ((), ())), preferred_element_type=jnp.float32
    )


def kernel(
    n_ctx, n_tp, group,
    feats_in, taps, residues, rates, skip, w_hbm, out,
    feats,
    halo, w, gath, prod, query, conv, filts, states, rep_rates, row_rates, row_coefs,
    entering, e_send, e_recv, acc,
    in_sem, w_sem, halo_sems, es_sems, er_sems, left_sems, right_sems, fwd_sems, recv_sems,
):
    me, z = lax.axis_index("ctx"), lax.axis_index("tp")
    rows, width = feats.shape[1], feats.shape[2]
    modes, filters = rates.shape
    blocks, chunks = width // LANES, rows // SPAN
    per = LANES // group

    load = pltpu.make_async_copy(feats_in, feats, in_sem)
    load.start()
    w_copy = pltpu.make_async_copy(w_hbm, w, w_sem)
    w_copy.start()

    barrier = pltpu.get_barrier_semaphore()

    def greet(d, _):
        pl.semaphore_signal(
            barrier, inc=1, device_id=(lax.rem(me + d, n_ctx), z), device_id_type=MESH
        )
        return 0

    lax.fori_loop(1, n_ctx, greet, 0)

    @pl.when(z > 0)
    def _():
        pl.semaphore_signal(barrier, inc=1, device_id=(me, z - 1), device_id_type=MESH)

    @pl.when(z < n_tp - 1)
    def _():
        pl.semaphore_signal(barrier, inc=1, device_id=(me, z + 1), device_id_type=MESH)

    pick = (iota((filters, width), 0) == iota((filters, width), 1) // group).astype(jnp.float32)

    def repeat(x):
        return lax.dot_general(
            x, pick, (((1,), (0,)), ((), ())),
            precision=lax.Precision.HIGHEST, preferred_element_type=jnp.float32,
        )

    diag = iota((modes, width), 0) == iota((modes, width), 1) % modes
    rep_rates[...] = repeat(rates[...])
    row_rates[...] = jnp.sum(jnp.where(diag, rep_rates[...], 0.0), axis=0, keepdims=True)
    row_res = jnp.sum(jnp.where(diag, repeat(residues[...]), 0.0), axis=0, keepdims=True)
    row_coefs[...] = row_res * jnp.sqrt(2.0 * row_rates[...])

    neighbours = (z > 0).astype(jnp.int32) + (z < n_tp - 1).astype(jnp.int32)
    pl.semaphore_wait(barrier, n_ctx - 1 + neighbours)

    halo_copy = pltpu.make_async_remote_copy(
        src_ref=feats_in.at[:, pl.ds(rows - HALO, HALO), :],
        dst_ref=halo,
        send_sem=halo_sems.at[0],
        recv_sem=halo_sems.at[1],
        device_id=(lax.rem(me + 1, n_ctx), z),
        device_id_type=MESH,
    )

    @pl.when(me < n_ctx - 1)
    def _():
        halo_copy.start()

    @pl.when(me == 0)
    def _():
        halo[...] = jnp.zeros_like(halo)

    def lanes_of(b):
        return pl.ds(pl.multiple_of(b * LANES, LANES), LANES)

    def filters_of(b, _):
        lanes = lanes_of(b)
        rate, coef = row_rates[:, lanes], row_coefs[:, lanes]
        at = iota((SPAN, LANES), 0).astype(jnp.float32)
        a_high, a_low = split(coef * jnp.exp(-rate * at))
        rise = jnp.exp(rate * at)
        rise_high = rise.astype(jnp.bfloat16).astype(jnp.float32)
        rise_low = rise - rise_high
        shape = (per * SPAN, LANES)
        own = iota(shape, 0) // SPAN == iota(shape, 1) // modes
        b_high = jnp.where(own, jnp.concatenate([rise_high] * per, 0), 0.0).astype(jnp.bfloat16)
        b_low = jnp.where(own, jnp.concatenate([rise_low] * per, 0), 0.0).astype(jnp.bfloat16)
        filt = (
            dot(a_high, b_high, (1, 1)) + dot(a_low, b_high, (1, 1)) + dot(a_high, b_low, (1, 1))
        )
        filts[b] = jnp.where(
            iota(filt.shape, 0) >= iota(filt.shape, 1) % SPAN, filt, 0.0
        ).astype(jnp.bfloat16)
        return 0

    lax.fori_loop(0, blocks, filters_of, 0)
    load.wait()

    @pl.when(me > 0)
    def _():
        halo_copy.wait_recv()

    def wide(x):
        return jnp.concatenate([x[k * SPAN : (k + 1) * SPAN] for k in range(chunks)], axis=1)

    def shorted(b, j):
        lanes = lanes_of(b)
        here = feats[j, :, lanes].astype(jnp.float32)
        before = halo[j, :, lanes].astype(jnp.float32)
        row = iota((rows, LANES), 0)
        last, second = before[HALO - 1 : HALO], before[HALO - 2 : HALO - 1]
        one = jnp.where(row == 0, last, pltpu.roll(here, 1, 0))
        two = jnp.where(row == 0, second, jnp.where(row == 1, last, pltpu.roll(here, 2, 0)))
        tap = [taps[s, pl.ds(j, 1), lanes] for s in range(3)]
        return tap[0] * here + tap[1] * one + tap[2] * two

    def first(b, _):
        lanes = lanes_of(b)
        query[b] = shorted(b, 0)
        product = shorted(b, 1) * shorted(b, 2)
        prod[b] = product
        rate = row_rates[:, lanes]
        left_over = (SPAN - iota((SPAN, LANES), 0)).astype(jnp.float32)
        high, low = split(jnp.exp(-rate * left_over))
        value = wide(product).astype(jnp.bfloat16)
        full = dot(high, value, (0, 0)) + dot(low, value, (0, 0))
        own = iota(full.shape, 0) // modes == (iota(full.shape, 1) % LANES) // group
        full = jnp.where(own, full, 0.0)
        state = full[:modes]
        for f in range(1, per):
            state = state + full[f * modes : (f + 1) * modes]
        states[b] = state
        decay = jnp.exp(-float(SPAN) * rep_rates[:, lanes])
        total = state[:, :LANES]
        for k in range(1, chunks):
            total = total * decay + state[:, k * LANES : (k + 1) * LANES]
        e_send[:, lanes] = total.astype(jnp.bfloat16)
        return 0

    lax.fori_loop(0, blocks, first, 0)

    def e_copy(d):
        return pltpu.make_async_remote_copy(
            src_ref=e_send,
            dst_ref=e_recv.at[d - 1],
            send_sem=es_sems.at[d - 1],
            recv_sem=er_sems.at[d - 1],
            device_id=(lax.rem(me + d, n_ctx), z),
            device_id_type=MESH,
        )

    def e_start(d, _):
        @pl.when(me + d < n_ctx)
        def _():
            e_copy(d).start()

        return 0

    lax.fori_loop(1, n_ctx, e_start, 0)

    def within(b, _):
        value = jnp.concatenate([wide(prod[b])] * per, 0)
        own = iota(value.shape, 0) // SPAN == (iota(value.shape, 1) % LANES) // group
        value = jnp.where(own, value, 0.0).astype(jnp.bfloat16)
        conv[b] = dot(filts[b], value, (1, 0))
        return 0

    ahead = min(AHEAD, blocks)
    lax.fori_loop(0, ahead, within, 0)

    entering[...] = jnp.zeros_like(entering)

    def e_take(d, _):
        @pl.when(me >= d)
        def _():
            e_copy(d).wait_recv()
            span = ((d - 1) * rows).astype(jnp.float32)
            entering[...] += jnp.exp(-span * rep_rates[...]) * e_recv[d - 1].astype(jnp.float32)

        return 0

    lax.fori_loop(1, n_ctx, e_take, 0)

    def own_copy(b, to, sems):
        return pltpu.make_async_remote_copy(
            src_ref=gath.at[z, b],
            dst_ref=gath.at[z, b],
            send_sem=sems.at[b],
            recv_sem=recv_sems.at[z, b],
            device_id=(me, to),
            device_id_type=MESH,
        )

    def finish(b, _):
        lanes = lanes_of(b)
        rate, coef = row_rates[:, lanes], row_coefs[:, lanes]
        at = iota((SPAN, LANES), 0).astype(jnp.float32)
        a_high, a_low = split(coef * jnp.exp(-rate * at))
        decay = jnp.exp(-float(SPAN) * rep_rates[:, lanes])
        held, parts, state = entering[:, lanes], [], states[b]
        for k in range(chunks):
            parts.append(held)
            held = held * decay + state[:, k * LANES : (k + 1) * LANES]
        tall = jnp.concatenate([jnp.concatenate(parts, axis=1)] * per, 0)
        own = iota(tall.shape, 0) // modes == (iota(tall.shape, 1) % LANES) // group
        tall = jnp.where(own, tall, 0.0).astype(jnp.bfloat16)
        total = conv[b] + dot(a_high, tall, (1, 0)) + dot(a_low, tall, (1, 0))
        direct = skip[:, lanes]
        for k in range(chunks):
            span = pl.ds(k * SPAN, SPAN)
            value = total[:, k * LANES : (k + 1) * LANES] + direct * prod[b, span, :]
            gath[z, b, span, :] = (query[b, span, :] * value).astype(jnp.bfloat16)

        @pl.when(z > 0)
        def _():
            own_copy(b, z - 1, left_sems).start()

        @pl.when(z < n_tp - 1)
        def _():
            own_copy(b, z + 1, right_sems).start()

        return 0

    def both(b, _):
        finish(b, 0)
        within(b + ahead, 0)
        return 0

    lax.fori_loop(0, blocks - ahead, both, 0)
    lax.fori_loop(blocks - ahead, blocks, finish, 0)

    def project(shard, p):
        left = jnp.concatenate([gath[shard, 2 * p], gath[shard, 2 * p + 1]], axis=1)
        depth = 2 * LANES
        at = pl.multiple_of(shard * width + p * depth, depth)
        acc[...] += dot(left, w[pl.ds(at, depth), :], (1, 0))

    w_copy.wait()
    acc[...] = jnp.zeros_like(acc)

    def own_step(p, _):
        project(z, p)
        return 0

    lax.fori_loop(0, blocks // 2, own_step, 0)

    def pass_copy(shard, b, to):
        return pltpu.make_async_remote_copy(
            src_ref=gath.at[shard, b],
            dst_ref=gath.at[shard, b],
            send_sem=fwd_sems.at[shard, b],
            recv_sem=recv_sems.at[shard, b],
            device_id=(me, to),
            device_id_type=MESH,
        )

    def hop(i, _):
        d, p = 1 + i // (blocks // 2), i % (blocks // 2)
        above, below = z + d, z - d
        for b in (2 * p, 2 * p + 1):
            @pl.when(above < n_tp)
            def _():
                pass_copy(above, b, lax.rem(z + 1, n_tp)).wait_recv()

                @pl.when(z > 0)
                def _():
                    pass_copy(above, b, z - 1).start()

            @pl.when(below >= 0)
            def _():
                pass_copy(below, b, lax.rem(z + 1, n_tp)).wait_recv()

                @pl.when(z < n_tp - 1)
                def _():
                    pass_copy(below, b, z + 1).start()

        @pl.when(above < n_tp)
        def _():
            project(above, p)

        @pl.when(below >= 0)
        def _():
            project(below, p)

        return 0

    lax.fori_loop(0, (n_tp - 1) * (blocks // 2), hop, 0)
    out[...] = acc[...].astype(out.dtype)

    @pl.when(me < n_ctx - 1)
    def _():
        halo_copy.wait_send()

    def e_sent(d, _):
        @pl.when(me + d < n_ctx)
        def _():
            e_copy(d).wait_send()

        return 0

    lax.fori_loop(1, n_ctx, e_sent, 0)

    def own_sent(b, _):
        @pl.when(z > 0)
        def _():
            own_copy(b, z - 1, left_sems).wait_send()

        @pl.when(z < n_tp - 1)
        def _():
            own_copy(b, z + 1, right_sems).wait_send()

        return 0

    lax.fori_loop(0, blocks, own_sent, 0)

    def pass_sent(i, _):
        shard, b = i // blocks, i % blocks

        @pl.when((shard > z) & (z > 0))
        def _():
            pass_copy(shard, b, z - 1).wait_send()

        @pl.when((shard < z) & (z < n_tp - 1))
        def _():
            pass_copy(shard, b, z + 1).wait_send()

        return 0

    lax.fori_loop(0, n_tp * blocks, pass_sent, 0)


def shards(n_ctx, n_tp, features, short_taps, residues, rates, skip, out_weight):
    rows, _, width = features.shape
    modes, filters = rates.shape
    group = width // filters
    blocks, chunks = width // LANES, rows // SPAN
    columns = out_weight.shape[1]
    vmem = pl.BlockSpec(memory_space=pltpu.VMEM)
    f32, bf16 = jnp.float32, jnp.bfloat16
    dma = pltpu.SemaphoreType.DMA
    return pl.pallas_call(
        functools.partial(kernel, n_ctx, n_tp, group),
        out_shape=jax.ShapeDtypeStruct((rows, columns), bf16),
        in_specs=[pl.BlockSpec(memory_space=pl.ANY)] + [vmem] * 4 + [pl.BlockSpec(memory_space=pl.ANY)],
        out_specs=vmem,
        scratch_shapes=[
            pltpu.VMEM((3, rows, width), bf16),
            pltpu.VMEM((3, HALO, width), bf16),
            pltpu.VMEM(out_weight.shape, bf16),
            pltpu.VMEM((n_tp, blocks, rows, LANES), bf16),
            pltpu.VMEM((blocks, rows, LANES), f32),
            pltpu.VMEM((blocks, rows, LANES), f32),
            pltpu.VMEM((blocks, SPAN, chunks * LANES), f32),
            pltpu.VMEM((blocks, SPAN, LANES // group * SPAN), bf16),
            pltpu.VMEM((blocks, modes, chunks * LANES), f32),
            pltpu.VMEM((modes, width), f32),
            pltpu.VMEM((1, width), f32),
            pltpu.VMEM((1, width), f32),
            pltpu.VMEM((modes, width), f32),
            pltpu.VMEM((modes, width), bf16),
            pltpu.VMEM((n_ctx - 1, modes, width), bf16),
            pltpu.VMEM((rows, columns), f32),
            dma(()),
            dma(()),
            dma((2,)),
            dma((n_ctx - 1,)),
            dma((n_ctx - 1,)),
            dma((blocks,)),
            dma((blocks,)),
            dma((n_tp, blocks)),
            dma((n_tp, blocks)),
        ],
        compiler_params=pltpu.CompilerParams(
            collective_id=0, has_side_effects=True, vmem_limit_bytes=63 * 1024 * 1024
        ),
        cost_estimate=pl.CostEstimate(
            flops=2 * rows * width * n_tp * columns,
            bytes_accessed=2 * out_weight.size,
            transcendentals=0,
        ),
    )(
        jnp.transpose(features, (1, 0, 2)), short_taps, residues, rates,
        skip.reshape(1, width), out_weight,
    )


def solution(mesh):
    in_specs = (
        P("ctx", None, "tp"),
        P(None, None, "tp"),
        P(None, "tp"),
        P(None, "tp"),
        P("tp"),
        P(None, "tp"),
    )
    n_ctx, n_tp = mesh.shape["ctx"], mesh.shape["tp"]
    return jax.shard_map(
        functools.partial(shards, n_ctx, n_tp),
        mesh=mesh, in_specs=in_specs, out_specs=P("ctx", "tp"), check_vma=False,
    )
```

```python
import functools

import jax
import jax.numpy as jnp
from jax import lax
from jax.experimental import pallas as pl
from jax.experimental.pallas import tpu as pltpu
from jax.sharding import PartitionSpec as P

MESH = pl.DeviceIdType.MESH
LANES = 128
SPAN = 64
AHEAD = 3
HALO = 16


def iota(shape, dim):
    return lax.broadcasted_iota(jnp.int32, shape, dim)


def split(x):
    high = x.astype(jnp.bfloat16)
    low = (x - high.astype(jnp.float32)).astype(jnp.bfloat16)
    return high, low


def dot(left, right, dims):
    return lax.dot_general(
        left, right, ((dims[:1], dims[1:]), ((), ())), preferred_element_type=jnp.float32
    )


def kernel(
    n_ctx, n_tp, group,
    feats_in, taps, residues, rates, skip, w_hbm, out,
    feats,
    halo, w, gath, prod, query, conv, filts, states, rep_rates, row_rates, row_coefs,
    entering, e_send, e_recv, acc,
    in_sem, w_sem, halo_sems, es_sems, er_sems, left_sems, right_sems, fwd_sems, recv_sems,
):
    me, z = lax.axis_index("ctx"), lax.axis_index("tp")
    rows, width = feats.shape[1], feats.shape[2]
    modes, filters = rates.shape
    blocks, chunks = width // LANES, rows // SPAN
    per = LANES // group

    load = pltpu.make_async_copy(feats_in, feats, in_sem)
    load.start()
    w_copy = pltpu.make_async_copy(w_hbm, w, w_sem)

    barrier = pltpu.get_barrier_semaphore()

    def greet(d, _):
        pl.semaphore_signal(
            barrier, inc=1, device_id=(lax.rem(me + d, n_ctx), z), device_id_type=MESH
        )
        return 0

    lax.fori_loop(1, n_ctx, greet, 0)

    @pl.when(z > 0)
    def _():
        pl.semaphore_signal(barrier, inc=1, device_id=(me, z - 1), device_id_type=MESH)

    @pl.when(z < n_tp - 1)
    def _():
        pl.semaphore_signal(barrier, inc=1, device_id=(me, z + 1), device_id_type=MESH)

    pick = (iota((filters, width), 0) == iota((filters, width), 1) // group).astype(jnp.float32)

    def repeat(x):
        return lax.dot_general(
            x, pick, (((1,), (0,)), ((), ())),
            precision=lax.Precision.HIGHEST, preferred_element_type=jnp.float32,
        )

    diag = iota((modes, width), 0) == iota((modes, width), 1) % modes
    rep_rates[...] = repeat(rates[...])
    row_rates[...] = jnp.sum(jnp.where(diag, rep_rates[...], 0.0), axis=0, keepdims=True)
    row_res = jnp.sum(jnp.where(diag, repeat(residues[...]), 0.0), axis=0, keepdims=True)
    row_coefs[...] = row_res * jnp.sqrt(2.0 * row_rates[...])

    neighbours = (z > 0).astype(jnp.int32) + (z < n_tp - 1).astype(jnp.int32)
    pl.semaphore_wait(barrier, n_ctx - 1 + neighbours)

    halo_copy = pltpu.make_async_remote_copy(
        src_ref=feats_in.at[:, pl.ds(rows - HALO, HALO), :],
        dst_ref=halo,
        send_sem=halo_sems.at[0],
        recv_sem=halo_sems.at[1],
        device_id=(lax.rem(me + 1, n_ctx), z),
        device_id_type=MESH,
    )

    @pl.when(me < n_ctx - 1)
    def _():
        halo_copy.start()

    @pl.when(me == 0)
    def _():
        halo[...] = jnp.zeros_like(halo)

    def lanes_of(b):
        return pl.ds(pl.multiple_of(b * LANES, LANES), LANES)

    def filters_of(b, _):
        lanes = lanes_of(b)
        rate, coef = row_rates[:, lanes], row_coefs[:, lanes]
        at = iota((SPAN, LANES), 0).astype(jnp.float32)
        a_high, a_low = split(coef * jnp.exp(-rate * at))
        rise = jnp.exp(rate * at)
        rise_high = rise.astype(jnp.bfloat16).astype(jnp.float32)
        rise_low = rise - rise_high
        shape = (per * SPAN, LANES)
        own = iota(shape, 0) // SPAN == iota(shape, 1) // modes
        b_high = jnp.where(own, jnp.concatenate([rise_high] * per, 0), 0.0).astype(jnp.bfloat16)
        b_low = jnp.where(own, jnp.concatenate([rise_low] * per, 0), 0.0).astype(jnp.bfloat16)
        filt = (
            dot(a_high, b_high, (1, 1)) + dot(a_low, b_high, (1, 1)) + dot(a_high, b_low, (1, 1))
        )
        filts[b] = jnp.where(
            iota(filt.shape, 0) >= iota(filt.shape, 1) % SPAN, filt, 0.0
        ).astype(jnp.bfloat16)
        return 0

    ahead = min(AHEAD, blocks)
    for b in range(ahead):
        filters_of(b, 0)
    load.wait()
    w_copy.start()

    @pl.when(me > 0)
    def _():
        halo_copy.wait_recv()

    def wide(x):
        return jnp.concatenate([x[k * SPAN : (k + 1) * SPAN] for k in range(chunks)], axis=1)

    def shorted(b, j):
        lanes = lanes_of(b)
        here = feats[j, :, lanes].astype(jnp.float32)
        before = halo[j, :, lanes].astype(jnp.float32)
        row = iota((rows, LANES), 0)
        last, second = before[HALO - 1 : HALO], before[HALO - 2 : HALO - 1]
        one = jnp.where(row == 0, last, pltpu.roll(here, 1, 0))
        two = jnp.where(row == 0, second, jnp.where(row == 1, last, pltpu.roll(here, 2, 0)))
        tap = [taps[s, pl.ds(j, 1), lanes] for s in range(3)]
        return tap[0] * here + tap[1] * one + tap[2] * two

    def first(b, _):
        lanes = lanes_of(b)
        product = shorted(b, 1) * shorted(b, 2)
        prod[b] = product
        rate = row_rates[:, lanes]
        left_over = (SPAN - iota((SPAN, LANES), 0)).astype(jnp.float32)
        high, low = split(jnp.exp(-rate * left_over))
        value = wide(product).astype(jnp.bfloat16)
        full = dot(high, value, (0, 0)) + dot(low, value, (0, 0))
        own = iota(full.shape, 0) // modes == (iota(full.shape, 1) % LANES) // group
        full = jnp.where(own, full, 0.0)
        state = full[:modes]
        for f in range(1, per):
            state = state + full[f * modes : (f + 1) * modes]
        states[b] = state
        decay = jnp.exp(-float(SPAN) * rep_rates[:, lanes])
        total = state[:, :LANES]
        for k in range(1, chunks):
            total = total * decay + state[:, k * LANES : (k + 1) * LANES]
        e_send[:, lanes] = total.astype(jnp.bfloat16)
        return 0

    for b in range(blocks):
        first(b, 0)

    def e_copy(d):
        return pltpu.make_async_remote_copy(
            src_ref=e_send,
            dst_ref=e_recv.at[d - 1],
            send_sem=es_sems.at[d - 1],
            recv_sem=er_sems.at[d - 1],
            device_id=(lax.rem(me + d, n_ctx), z),
            device_id_type=MESH,
        )

    def e_start(d, _):
        @pl.when(me + d < n_ctx)
        def _():
            e_copy(d).start()

        return 0

    lax.fori_loop(1, n_ctx, e_start, 0)

    def within(b, _):
        query[b] = shorted(b, 0)
        value = jnp.concatenate([wide(prod[b])] * per, 0)
        own = iota(value.shape, 0) // SPAN == (iota(value.shape, 1) % LANES) // group
        value = jnp.where(own, value, 0.0).astype(jnp.bfloat16)
        conv[b] = dot(filts[b], value, (1, 0))
        return 0

    for b in range(ahead):
        within(b, 0)

    entering[...] = jnp.zeros_like(entering)

    def e_take(d, _):
        @pl.when(me >= d)
        def _():
            e_copy(d).wait_recv()
            span = ((d - 1) * rows).astype(jnp.float32)
            entering[...] += jnp.exp(-span * rep_rates[...]) * e_recv[d - 1].astype(jnp.float32)

        return 0

    lax.fori_loop(1, n_ctx, e_take, 0)

    def own_copy(b, to, sems):
        return pltpu.make_async_remote_copy(
            src_ref=gath.at[z, b],
            dst_ref=gath.at[z, b],
            send_sem=sems.at[b],
            recv_sem=recv_sems.at[z, b],
            device_id=(me, to),
            device_id_type=MESH,
        )

    def finish(b, _):
        lanes = lanes_of(b)
        rate, coef = row_rates[:, lanes], row_coefs[:, lanes]
        at = iota((SPAN, LANES), 0).astype(jnp.float32)
        a_high, a_low = split(coef * jnp.exp(-rate * at))
        decay = jnp.exp(-float(SPAN) * rep_rates[:, lanes])
        held, parts, state = entering[:, lanes], [], states[b]
        for k in range(chunks):
            parts.append(held)
            held = held * decay + state[:, k * LANES : (k + 1) * LANES]
        tall = jnp.concatenate([jnp.concatenate(parts, axis=1)] * per, 0)
        own = iota(tall.shape, 0) // modes == (iota(tall.shape, 1) % LANES) // group
        tall = jnp.where(own, tall, 0.0).astype(jnp.bfloat16)
        total = conv[b] + dot(a_high, tall, (1, 0)) + dot(a_low, tall, (1, 0))
        direct = skip[:, lanes]
        for k in range(chunks):
            span = pl.ds(k * SPAN, SPAN)
            value = total[:, k * LANES : (k + 1) * LANES] + direct * prod[b, span, :]
            gath[z, b, span, :] = (query[b, span, :] * value).astype(jnp.bfloat16)

        @pl.when(z > 0)
        def _():
            own_copy(b, z - 1, left_sems).start()

        @pl.when(z < n_tp - 1)
        def _():
            own_copy(b, z + 1, right_sems).start()

        return 0

    def both(b, _):
        filters_of(b + ahead, 0)
        finish(b, 0)
        within(b + ahead, 0)
        return 0

    lax.fori_loop(0, blocks - ahead, both, 0)
    lax.fori_loop(blocks - ahead, blocks, finish, 0)

    def project(shard, p):
        left = jnp.concatenate([gath[shard, 2 * p], gath[shard, 2 * p + 1]], axis=1)
        depth = 2 * LANES
        at = pl.multiple_of(shard * width + p * depth, depth)
        acc[...] += dot(left, w[pl.ds(at, depth), :], (1, 0))

    w_copy.wait()
    acc[...] = jnp.zeros_like(acc)

    def own_step(p, _):
        project(z, p)
        return 0

    lax.fori_loop(0, blocks // 2, own_step, 0)

    def pass_copy(shard, b, to):
        return pltpu.make_async_remote_copy(
            src_ref=gath.at[shard, b],
            dst_ref=gath.at[shard, b],
            send_sem=fwd_sems.at[shard, b],
            recv_sem=recv_sems.at[shard, b],
            device_id=(me, to),
            device_id_type=MESH,
        )

    def hop(i, _):
        d, p = 1 + i // (blocks // 2), i % (blocks // 2)
        above, below = z + d, z - d
        for b in (2 * p, 2 * p + 1):
            @pl.when(above < n_tp)
            def _():
                pass_copy(above, b, lax.rem(z + 1, n_tp)).wait_recv()

                @pl.when(z > 0)
                def _():
                    pass_copy(above, b, z - 1).start()

            @pl.when(below >= 0)
            def _():
                pass_copy(below, b, lax.rem(z + 1, n_tp)).wait_recv()

                @pl.when(z < n_tp - 1)
                def _():
                    pass_copy(below, b, z + 1).start()

        @pl.when(above < n_tp)
        def _():
            project(above, p)

        @pl.when(below >= 0)
        def _():
            project(below, p)

        return 0

    lax.fori_loop(0, (n_tp - 1) * (blocks // 2), hop, 0)
    out[...] = acc[...].astype(out.dtype)

    @pl.when(me < n_ctx - 1)
    def _():
        halo_copy.wait_send()

    def e_sent(d, _):
        @pl.when(me + d < n_ctx)
        def _():
            e_copy(d).wait_send()

        return 0

    lax.fori_loop(1, n_ctx, e_sent, 0)

    def own_sent(b, _):
        @pl.when(z > 0)
        def _():
            own_copy(b, z - 1, left_sems).wait_send()

        @pl.when(z < n_tp - 1)
        def _():
            own_copy(b, z + 1, right_sems).wait_send()

        return 0

    lax.fori_loop(0, blocks, own_sent, 0)

    def pass_sent(i, _):
        shard, b = i // blocks, i % blocks

        @pl.when((shard > z) & (z > 0))
        def _():
            pass_copy(shard, b, z - 1).wait_send()

        @pl.when((shard < z) & (z < n_tp - 1))
        def _():
            pass_copy(shard, b, z + 1).wait_send()

        return 0

    lax.fori_loop(0, n_tp * blocks, pass_sent, 0)


def shards(n_ctx, n_tp, features, short_taps, residues, rates, skip, out_weight):
    rows, _, width = features.shape
    modes, filters = rates.shape
    group = width // filters
    blocks, chunks = width // LANES, rows // SPAN
    columns = out_weight.shape[1]
    vmem = pl.BlockSpec(memory_space=pltpu.VMEM)
    f32, bf16 = jnp.float32, jnp.bfloat16
    dma = pltpu.SemaphoreType.DMA
    return pl.pallas_call(
        functools.partial(kernel, n_ctx, n_tp, group),
        out_shape=jax.ShapeDtypeStruct((rows, columns), bf16),
        in_specs=[pl.BlockSpec(memory_space=pl.ANY)] + [vmem] * 4 + [pl.BlockSpec(memory_space=pl.ANY)],
        out_specs=vmem,
        scratch_shapes=[
            pltpu.VMEM((3, rows, width), bf16),
            pltpu.VMEM((3, HALO, width), bf16),
            pltpu.VMEM(out_weight.shape, bf16),
            pltpu.VMEM((n_tp, blocks, rows, LANES), bf16),
            pltpu.VMEM((blocks, rows, LANES), f32),
            pltpu.VMEM((blocks, rows, LANES), f32),
            pltpu.VMEM((blocks, SPAN, chunks * LANES), f32),
            pltpu.VMEM((blocks, SPAN, LANES // group * SPAN), bf16),
            pltpu.VMEM((blocks, modes, chunks * LANES), f32),
            pltpu.VMEM((modes, width), f32),
            pltpu.VMEM((1, width), f32),
            pltpu.VMEM((1, width), f32),
            pltpu.VMEM((modes, width), f32),
            pltpu.VMEM((modes, width), bf16),
            pltpu.VMEM((n_ctx - 1, modes, width), bf16),
            pltpu.VMEM((rows, columns), f32),
            dma(()),
            dma(()),
            dma((2,)),
            dma((n_ctx - 1,)),
            dma((n_ctx - 1,)),
            dma((blocks,)),
            dma((blocks,)),
            dma((n_tp, blocks)),
            dma((n_tp, blocks)),
        ],
        compiler_params=pltpu.CompilerParams(
            collective_id=0, has_side_effects=True, vmem_limit_bytes=63 * 1024 * 1024
        ),
        cost_estimate=pl.CostEstimate(
            flops=2 * rows * width * n_tp * columns,
            bytes_accessed=2 * out_weight.size,
            transcendentals=0,
        ),
    )(
        jnp.transpose(features, (1, 0, 2)), short_taps, residues, rates,
        skip.reshape(1, width), out_weight,
    )


def solution(mesh):
    in_specs = (
        P("ctx", None, "tp"),
        P(None, None, "tp"),
        P(None, "tp"),
        P(None, "tp"),
        P("tp"),
        P(None, "tp"),
    )
    n_ctx, n_tp = mesh.shape["ctx"], mesh.shape["tp"]
    return jax.shard_map(
        functools.partial(shards, n_ctx, n_tp),
        mesh=mesh, in_specs=in_specs, out_specs=P("ctx", "tp"), check_vma=False,
    )
```

```python
import functools

import jax
import jax.numpy as jnp
from jax import lax
from jax.experimental import pallas as pl
from jax.experimental.pallas import tpu as pltpu
from jax.sharding import PartitionSpec as P

MESH = pl.DeviceIdType.MESH
LANES = 128
SPAN = 64
AHEAD = 3
HALO = 16


def iota(shape, dim):
    return lax.broadcasted_iota(jnp.int32, shape, dim)


def split(x):
    high = x.astype(jnp.bfloat16)
    low = (x - high.astype(jnp.float32)).astype(jnp.bfloat16)
    return high, low


def dot(left, right, dims):
    return lax.dot_general(
        left, right, ((dims[:1], dims[1:]), ((), ())), preferred_element_type=jnp.float32
    )


def kernel(
    n_ctx, n_tp, group,
    feats_in, taps, residues, rates, skip, w_hbm, out,
    feats,
    halo, w, gath, prod, query, conv, filts, states, rep_rates, row_rates, row_coefs,
    entering, e_send, e_recv, acc,
    in_sem, w_sem, halo_sems, es_sems, er_sems, left_sems, right_sems, fwd_sems, recv_sems,
):
    me, z = lax.axis_index("ctx"), lax.axis_index("tp")
    rows, width = feats.shape[1], feats.shape[2]
    modes, filters = rates.shape
    blocks, chunks = width // LANES, rows // SPAN
    per = LANES // group

    load = pltpu.make_async_copy(feats_in, feats, in_sem)
    load.start()
    w_copy = pltpu.make_async_copy(w_hbm, w, w_sem)

    barrier = pltpu.get_barrier_semaphore()

    def greet(d, _):
        pl.semaphore_signal(
            barrier, inc=1, device_id=(lax.rem(me + d, n_ctx), z), device_id_type=MESH
        )
        return 0

    lax.fori_loop(1, n_ctx, greet, 0)

    @pl.when(z > 0)
    def _():
        pl.semaphore_signal(barrier, inc=1, device_id=(me, z - 1), device_id_type=MESH)

    @pl.when(z < n_tp - 1)
    def _():
        pl.semaphore_signal(barrier, inc=1, device_id=(me, z + 1), device_id_type=MESH)

    pick = (iota((filters, width), 0) == iota((filters, width), 1) // group).astype(jnp.float32)

    def repeat(x):
        return lax.dot_general(
            x, pick, (((1,), (0,)), ((), ())),
            precision=lax.Precision.HIGHEST, preferred_element_type=jnp.float32,
        )

    diag = iota((modes, width), 0) == iota((modes, width), 1) % modes
    rep_rates[...] = repeat(rates[...])
    row_rates[...] = jnp.sum(jnp.where(diag, rep_rates[...], 0.0), axis=0, keepdims=True)
    row_res = jnp.sum(jnp.where(diag, repeat(residues[...]), 0.0), axis=0, keepdims=True)
    row_coefs[...] = row_res * jnp.sqrt(2.0 * row_rates[...])

    neighbours = (z > 0).astype(jnp.int32) + (z < n_tp - 1).astype(jnp.int32)
    pl.semaphore_wait(barrier, n_ctx - 1 + neighbours)

    halo_copy = pltpu.make_async_remote_copy(
        src_ref=feats_in.at[:, pl.ds(rows - HALO, HALO), :],
        dst_ref=halo,
        send_sem=halo_sems.at[0],
        recv_sem=halo_sems.at[1],
        device_id=(lax.rem(me + 1, n_ctx), z),
        device_id_type=MESH,
    )

    @pl.when(me < n_ctx - 1)
    def _():
        halo_copy.start()

    @pl.when(me == 0)
    def _():
        halo[...] = jnp.zeros_like(halo)

    def lanes_of(b):
        return pl.ds(pl.multiple_of(b * LANES, LANES), LANES)

    def filters_of(b, _):
        lanes = lanes_of(b)
        rate, coef = row_rates[:, lanes], row_coefs[:, lanes]
        at = iota((SPAN, LANES), 0).astype(jnp.float32)
        a_high, a_low = split(coef * jnp.exp(-rate * at))
        rise = jnp.exp(rate * at)
        rise_high = rise.astype(jnp.bfloat16).astype(jnp.float32)
        rise_low = rise - rise_high
        shape = (per * SPAN, LANES)
        own = iota(shape, 0) // SPAN == iota(shape, 1) // modes
        b_high = jnp.where(own, jnp.concatenate([rise_high] * per, 0), 0.0).astype(jnp.bfloat16)
        b_low = jnp.where(own, jnp.concatenate([rise_low] * per, 0), 0.0).astype(jnp.bfloat16)
        filt = (
            dot(a_high, b_high, (1, 1)) + dot(a_low, b_high, (1, 1)) + dot(a_high, b_low, (1, 1))
        )
        filts[b] = jnp.where(
            iota(filt.shape, 0) >= iota(filt.shape, 1) % SPAN, filt, 0.0
        ).astype(jnp.bfloat16)
        return 0

    ahead = min(AHEAD, blocks)
    for b in range(ahead):
        filters_of(b, 0)
    load.wait()
    w_copy.start()

    @pl.when(me > 0)
    def _():
        halo_copy.wait_recv()

    def wide(x):
        return jnp.concatenate([x[k * SPAN : (k + 1) * SPAN] for k in range(chunks)], axis=1)

    def shorted(b, j):
        lanes = lanes_of(b)
        here = feats[j, :, lanes].astype(jnp.float32)
        before = halo[j, :, lanes].astype(jnp.float32)
        row = iota((rows, LANES), 0)
        last, second = before[HALO - 1 : HALO], before[HALO - 2 : HALO - 1]
        one = jnp.where(row == 0, last, pltpu.roll(here, 1, 0))
        two = jnp.where(row == 0, second, jnp.where(row == 1, last, pltpu.roll(here, 2, 0)))
        tap = [taps[s, pl.ds(j, 1), lanes] for s in range(3)]
        return tap[0] * here + tap[1] * one + tap[2] * two

    def first(b, _):
        lanes = lanes_of(b)
        product = shorted(b, 1) * shorted(b, 2)
        prod[b] = product
        rate = row_rates[:, lanes]
        left_over = (SPAN - iota((SPAN, LANES), 0)).astype(jnp.float32)
        high, low = split(jnp.exp(-rate * left_over))
        value = wide(product).astype(jnp.bfloat16)
        full = dot(high, value, (0, 0)) + dot(low, value, (0, 0))
        own = iota(full.shape, 0) // modes == (iota(full.shape, 1) % LANES) // group
        full = jnp.where(own, full, 0.0)
        state = full[:modes]
        for f in range(1, per):
            state = state + full[f * modes : (f + 1) * modes]
        states[b] = state
        decay = jnp.exp(-float(SPAN) * rep_rates[:, lanes])
        total = state[:, :LANES]
        for k in range(1, chunks):
            total = total * decay + state[:, k * LANES : (k + 1) * LANES]
        e_send[:, lanes] = total.astype(jnp.bfloat16)
        return 0

    for b in range(blocks):
        first(b, 0)

    def e_copy(d):
        return pltpu.make_async_remote_copy(
            src_ref=e_send,
            dst_ref=e_recv.at[d - 1],
            send_sem=es_sems.at[d - 1],
            recv_sem=er_sems.at[d - 1],
            device_id=(lax.rem(me + d, n_ctx), z),
            device_id_type=MESH,
        )

    def e_start(d, _):
        @pl.when(me + d < n_ctx)
        def _():
            e_copy(d).start()

        return 0

    lax.fori_loop(1, n_ctx, e_start, 0)

    def within(b, _):
        query[b] = shorted(b, 0)
        value = jnp.concatenate([wide(prod[b])] * per, 0)
        own = iota(value.shape, 0) // SPAN == (iota(value.shape, 1) % LANES) // group
        value = jnp.where(own, value, 0.0).astype(jnp.bfloat16)
        conv[b] = dot(filts[b], value, (1, 0))
        return 0

    for b in range(ahead):
        within(b, 0)

    entering[...] = jnp.zeros_like(entering)

    def e_take(d, _):
        @pl.when(me >= d)
        def _():
            e_copy(d).wait_recv()
            span = ((d - 1) * rows).astype(jnp.float32)
            entering[...] += jnp.exp(-span * rep_rates[...]) * e_recv[d - 1].astype(jnp.float32)

        return 0

    lax.fori_loop(1, n_ctx, e_take, 0)

    def own_copy(b, to, sems):
        return pltpu.make_async_remote_copy(
            src_ref=gath.at[z, b],
            dst_ref=gath.at[z, b],
            send_sem=sems.at[b],
            recv_sem=recv_sems.at[z, b],
            device_id=(me, to),
            device_id_type=MESH,
        )

    def finish(b, _):
        lanes = lanes_of(b)
        rate, coef = row_rates[:, lanes], row_coefs[:, lanes]
        at = iota((SPAN, LANES), 0).astype(jnp.float32)
        a_high, a_low = split(coef * jnp.exp(-rate * at))
        decay = jnp.exp(-float(SPAN) * rep_rates[:, lanes])
        held, parts, state = entering[:, lanes], [], states[b]
        for k in range(chunks):
            parts.append(held)
            held = held * decay + state[:, k * LANES : (k + 1) * LANES]
        tall = jnp.concatenate([jnp.concatenate(parts, axis=1)] * per, 0)
        own = iota(tall.shape, 0) // modes == (iota(tall.shape, 1) % LANES) // group
        tall = jnp.where(own, tall, 0.0).astype(jnp.bfloat16)
        total = conv[b] + dot(a_high, tall, (1, 0)) + dot(a_low, tall, (1, 0))
        direct = skip[:, lanes]
        for k in range(chunks):
            span = pl.ds(k * SPAN, SPAN)
            value = total[:, k * LANES : (k + 1) * LANES] + direct * prod[b, span, :]
            gath[z, b, span, :] = (query[b, span, :] * value).astype(jnp.bfloat16)

        @pl.when(z > 0)
        def _():
            own_copy(b, z - 1, left_sems).start()

        @pl.when(z < n_tp - 1)
        def _():
            own_copy(b, z + 1, right_sems).start()

        return 0

    def both(b, _):
        filters_of(b + ahead, 0)
        finish(b, 0)
        within(b + ahead, 0)
        return 0

    lax.fori_loop(0, blocks - ahead, both, 0)
    lax.fori_loop(blocks - ahead, blocks, finish, 0)

    def project(shard, p):
        left = jnp.concatenate([gath[shard, 2 * p], gath[shard, 2 * p + 1]], axis=1)
        depth = 2 * LANES
        at = pl.multiple_of(shard * width + p * depth, depth)
        acc[...] += dot(left, w[pl.ds(at, depth), :], (1, 0))

    w_copy.wait()
    acc[...] = jnp.zeros_like(acc)

    def own_step(p, _):
        project(z, p)
        return 0

    def pass_copy(shard, b, to):
        return pltpu.make_async_remote_copy(
            src_ref=gath.at[shard, b],
            dst_ref=gath.at[shard, b],
            send_sem=fwd_sems.at[shard, b],
            recv_sem=recv_sems.at[shard, b],
            device_id=(me, to),
            device_id_type=MESH,
        )

    def hop(i, _):
        d, p = 1 + i // (blocks // 2), i % (blocks // 2)
        above, below = z + d, z - d
        for b in (2 * p, 2 * p + 1):
            @pl.when(above < n_tp)
            def _():
                pass_copy(above, b, lax.rem(z + 1, n_tp)).wait_recv()

                @pl.when(z > 0)
                def _():
                    pass_copy(above, b, z - 1).start()

            @pl.when(below >= 0)
            def _():
                pass_copy(below, b, lax.rem(z + 1, n_tp)).wait_recv()

                @pl.when(z < n_tp - 1)
                def _():
                    pass_copy(below, b, z + 1).start()

        @pl.when(above < n_tp)
        def _():
            project(above, p)

        @pl.when(below >= 0)
        def _():
            project(below, p)

        return 0

    lax.fori_loop(0, blocks // 2, hop, 0)
    lax.fori_loop(0, blocks // 2, own_step, 0)
    lax.fori_loop(blocks // 2, (n_tp - 1) * (blocks // 2), hop, 0)
    out[...] = acc[...].astype(out.dtype)

    @pl.when(me < n_ctx - 1)
    def _():
        halo_copy.wait_send()

    def e_sent(d, _):
        @pl.when(me + d < n_ctx)
        def _():
            e_copy(d).wait_send()

        return 0

    lax.fori_loop(1, n_ctx, e_sent, 0)

    def own_sent(b, _):
        @pl.when(z > 0)
        def _():
            own_copy(b, z - 1, left_sems).wait_send()

        @pl.when(z < n_tp - 1)
        def _():
            own_copy(b, z + 1, right_sems).wait_send()

        return 0

    lax.fori_loop(0, blocks, own_sent, 0)

    def pass_sent(i, _):
        shard, b = i // blocks, i % blocks

        @pl.when((shard > z) & (z > 0))
        def _():
            pass_copy(shard, b, z - 1).wait_send()

        @pl.when((shard < z) & (z < n_tp - 1))
        def _():
            pass_copy(shard, b, z + 1).wait_send()

        return 0

    lax.fori_loop(0, n_tp * blocks, pass_sent, 0)


def shards(n_ctx, n_tp, features, short_taps, residues, rates, skip, out_weight):
    rows, _, width = features.shape
    modes, filters = rates.shape
    group = width // filters
    blocks, chunks = width // LANES, rows // SPAN
    columns = out_weight.shape[1]
    vmem = pl.BlockSpec(memory_space=pltpu.VMEM)
    f32, bf16 = jnp.float32, jnp.bfloat16
    dma = pltpu.SemaphoreType.DMA
    return pl.pallas_call(
        functools.partial(kernel, n_ctx, n_tp, group),
        out_shape=jax.ShapeDtypeStruct((rows, columns), bf16),
        in_specs=[pl.BlockSpec(memory_space=pl.ANY)] + [vmem] * 4 + [pl.BlockSpec(memory_space=pl.ANY)],
        out_specs=vmem,
        scratch_shapes=[
            pltpu.VMEM((3, rows, width), bf16),
            pltpu.VMEM((3, HALO, width), bf16),
            pltpu.VMEM(out_weight.shape, bf16),
            pltpu.VMEM((n_tp, blocks, rows, LANES), bf16),
            pltpu.VMEM((blocks, rows, LANES), f32),
            pltpu.VMEM((blocks, rows, LANES), f32),
            pltpu.VMEM((blocks, SPAN, chunks * LANES), f32),
            pltpu.VMEM((blocks, SPAN, LANES // group * SPAN), bf16),
            pltpu.VMEM((blocks, modes, chunks * LANES), f32),
            pltpu.VMEM((modes, width), f32),
            pltpu.VMEM((1, width), f32),
            pltpu.VMEM((1, width), f32),
            pltpu.VMEM((modes, width), f32),
            pltpu.VMEM((modes, width), bf16),
            pltpu.VMEM((n_ctx - 1, modes, width), bf16),
            pltpu.VMEM((rows, columns), f32),
            dma(()),
            dma(()),
            dma((2,)),
            dma((n_ctx - 1,)),
            dma((n_ctx - 1,)),
            dma((blocks,)),
            dma((blocks,)),
            dma((n_tp, blocks)),
            dma((n_tp, blocks)),
        ],
        compiler_params=pltpu.CompilerParams(
            collective_id=0, has_side_effects=True, vmem_limit_bytes=63 * 1024 * 1024
        ),
        cost_estimate=pl.CostEstimate(
            flops=2 * rows * width * n_tp * columns,
            bytes_accessed=2 * out_weight.size,
            transcendentals=0,
        ),
    )(
        jnp.transpose(features, (1, 0, 2)), short_taps, residues, rates,
        skip.reshape(1, width), out_weight,
    )


def solution(mesh):
    in_specs = (
        P("ctx", None, "tp"),
        P(None, None, "tp"),
        P(None, "tp"),
        P(None, "tp"),
        P("tp"),
        P(None, "tp"),
    )
    n_ctx, n_tp = mesh.shape["ctx"], mesh.shape["tp"]
    return jax.shard_map(
        functools.partial(shards, n_ctx, n_tp),
        mesh=mesh, in_specs=in_specs, out_specs=P("ctx", "tp"), check_vma=False,
    )
```

```python
import functools

import jax
import jax.numpy as jnp
from jax import lax
from jax.experimental import pallas as pl
from jax.experimental.pallas import tpu as pltpu
from jax.sharding import PartitionSpec as P

MESH = pl.DeviceIdType.MESH
LANES = 128
SPAN = 64
AHEAD = 3
HALO = 16


def iota(shape, dim):
    return lax.broadcasted_iota(jnp.int32, shape, dim)


def split(x):
    high = x.astype(jnp.bfloat16)
    low = (x - high.astype(jnp.float32)).astype(jnp.bfloat16)
    return high, low


def dot(left, right, dims):
    return lax.dot_general(
        left, right, ((dims[:1], dims[1:]), ((), ())), preferred_element_type=jnp.float32
    )


def kernel(
    n_ctx, n_tp, group,
    feats_in, taps, residues, rates, skip, w_hbm, out,
    feats,
    halo, w, gath, prod, query, conv, filts, states, rep_rates, row_rates, row_coefs,
    entering, e_send, e_recv, acc,
    in_sem, w_sem, halo_sems, es_sems, er_sems, left_sems, right_sems, fwd_sems, recv_sems,
):
    me, z = lax.axis_index("ctx"), lax.axis_index("tp")
    rows, width = feats.shape[1], feats.shape[2]
    modes, filters = rates.shape
    blocks, chunks = width // LANES, rows // SPAN
    per = LANES // group

    load = pltpu.make_async_copy(feats_in, feats, in_sem)
    load.start()
    w_copy = pltpu.make_async_copy(w_hbm, w, w_sem)

    barrier = pltpu.get_barrier_semaphore()

    def greet(d, _):
        pl.semaphore_signal(
            barrier, inc=1, device_id=(lax.rem(me + d, n_ctx), z), device_id_type=MESH
        )
        return 0

    lax.fori_loop(1, n_ctx, greet, 0)

    @pl.when(z > 0)
    def _():
        pl.semaphore_signal(barrier, inc=1, device_id=(me, z - 1), device_id_type=MESH)

    @pl.when(z < n_tp - 1)
    def _():
        pl.semaphore_signal(barrier, inc=1, device_id=(me, z + 1), device_id_type=MESH)

    pick = (iota((filters, width), 0) == iota((filters, width), 1) // group).astype(jnp.float32)

    def repeat(x):
        return lax.dot_general(
            x, pick, (((1,), (0,)), ((), ())),
            precision=lax.Precision.HIGHEST, preferred_element_type=jnp.float32,
        )

    diag = iota((modes, width), 0) == iota((modes, width), 1) % modes
    rep_rates[...] = repeat(rates[...])
    row_rates[...] = jnp.sum(jnp.where(diag, rep_rates[...], 0.0), axis=0, keepdims=True)
    row_res = jnp.sum(jnp.where(diag, repeat(residues[...]), 0.0), axis=0, keepdims=True)
    row_coefs[...] = row_res * jnp.sqrt(2.0 * row_rates[...])

    neighbours = (z > 0).astype(jnp.int32) + (z < n_tp - 1).astype(jnp.int32)
    pl.semaphore_wait(barrier, n_ctx - 1 + neighbours)

    halo_copy = pltpu.make_async_remote_copy(
        src_ref=feats_in.at[:, pl.ds(rows - HALO, HALO), :],
        dst_ref=halo,
        send_sem=halo_sems.at[0],
        recv_sem=halo_sems.at[1],
        device_id=(lax.rem(me + 1, n_ctx), z),
        device_id_type=MESH,
    )

    @pl.when(me < n_ctx - 1)
    def _():
        halo_copy.start()

    @pl.when(me == 0)
    def _():
        halo[...] = jnp.zeros_like(halo)

    def lanes_of(b):
        return pl.ds(pl.multiple_of(b * LANES, LANES), LANES)

    def filters_of(b, _):
        lanes = lanes_of(b)
        rate, coef = row_rates[:, lanes], row_coefs[:, lanes]
        at = iota((SPAN, LANES), 0).astype(jnp.float32)
        a_high, a_low = split(coef * jnp.exp(-rate * at))
        rise = jnp.exp(rate * at)
        rise_high = rise.astype(jnp.bfloat16).astype(jnp.float32)
        rise_low = rise - rise_high
        shape = (per * SPAN, LANES)
        own = iota(shape, 0) // SPAN == iota(shape, 1) // modes
        b_high = jnp.where(own, jnp.concatenate([rise_high] * per, 0), 0.0).astype(jnp.bfloat16)
        b_low = jnp.where(own, jnp.concatenate([rise_low] * per, 0), 0.0).astype(jnp.bfloat16)
        filt = (
            dot(a_high, b_high, (1, 1)) + dot(a_low, b_high, (1, 1)) + dot(a_high, b_low, (1, 1))
        )
        filts[b] = jnp.where(
            iota(filt.shape, 0) >= iota(filt.shape, 1) % SPAN, filt, 0.0
        ).astype(jnp.bfloat16)
        return 0

    ahead = min(AHEAD, blocks)
    for b in range(ahead):
        filters_of(b, 0)
    load.wait()
    w_copy.start()

    @pl.when(me > 0)
    def _():
        halo_copy.wait_recv()

    def wide(x):
        return jnp.concatenate([x[k * SPAN : (k + 1) * SPAN] for k in range(chunks)], axis=1)

    def shorted(b, j):
        lanes = lanes_of(b)
        here = feats[j, :, lanes].astype(jnp.float32)
        before = halo[j, :, lanes].astype(jnp.float32)
        row = iota((rows, LANES), 0)
        last, second = before[HALO - 1 : HALO], before[HALO - 2 : HALO - 1]
        one = jnp.where(row == 0, last, pltpu.roll(here, 1, 0))
        two = jnp.where(row == 0, second, jnp.where(row == 1, last, pltpu.roll(here, 2, 0)))
        tap = [taps[s, pl.ds(j, 1), lanes] for s in range(3)]
        return tap[0] * here + tap[1] * one + tap[2] * two

    def first(b, _):
        lanes = lanes_of(b)
        product = shorted(b, 1) * shorted(b, 2)
        prod[b] = product
        rate = row_rates[:, lanes]
        left_over = (SPAN - iota((SPAN, LANES), 0)).astype(jnp.float32)
        high, low = split(jnp.exp(-rate * left_over))
        value = wide(product).astype(jnp.bfloat16)
        full = dot(high, value, (0, 0)) + dot(low, value, (0, 0))
        own = iota(full.shape, 0) // modes == (iota(full.shape, 1) % LANES) // group
        full = jnp.where(own, full, 0.0)
        state = full[:modes]
        for f in range(1, per):
            state = state + full[f * modes : (f + 1) * modes]
        states[b] = state
        decay = jnp.exp(-float(SPAN) * rep_rates[:, lanes])
        total = state[:, :LANES]
        for k in range(1, chunks):
            total = total * decay + state[:, k * LANES : (k + 1) * LANES]
        e_send[:, lanes] = total.astype(jnp.bfloat16)
        return 0

    for b in range(blocks):
        first(b, 0)

    def e_copy(d):
        return pltpu.make_async_remote_copy(
            src_ref=e_send,
            dst_ref=e_recv.at[d - 1],
            send_sem=es_sems.at[d - 1],
            recv_sem=er_sems.at[d - 1],
            device_id=(lax.rem(me + d, n_ctx), z),
            device_id_type=MESH,
        )

    def e_start(d, _):
        @pl.when(me + d < n_ctx)
        def _():
            e_copy(d).start()

        return 0

    lax.fori_loop(1, n_ctx, e_start, 0)

    def within(b, _):
        query[b] = shorted(b, 0)
        value = jnp.concatenate([wide(prod[b])] * per, 0)
        own = iota(value.shape, 0) // SPAN == (iota(value.shape, 1) % LANES) // group
        value = jnp.where(own, value, 0.0).astype(jnp.bfloat16)
        conv[b] = dot(filts[b], value, (1, 0))
        return 0

    for b in range(ahead):
        within(b, 0)

    entering[...] = jnp.zeros_like(entering)

    def e_take(d, _):
        @pl.when(me >= d)
        def _():
            e_copy(d).wait_recv()
            span = ((d - 1) * rows).astype(jnp.float32)
            entering[...] += jnp.exp(-span * rep_rates[...]) * e_recv[d - 1].astype(jnp.float32)

        return 0

    lax.fori_loop(1, n_ctx, e_take, 0)

    def own_copy(b, to, sems):
        return pltpu.make_async_remote_copy(
            src_ref=gath.at[z, b],
            dst_ref=gath.at[z, b],
            send_sem=sems.at[b],
            recv_sem=recv_sems.at[z, b],
            device_id=(me, to),
            device_id_type=MESH,
        )

    def finish(b, _):
        lanes = lanes_of(b)
        rate, coef = row_rates[:, lanes], row_coefs[:, lanes]
        at = iota((SPAN, LANES), 0).astype(jnp.float32)
        a_high, a_low = split(coef * jnp.exp(-rate * at))
        decay = jnp.exp(-float(SPAN) * rep_rates[:, lanes])
        held, parts, state = entering[:, lanes], [], states[b]
        for k in range(chunks):
            parts.append(held)
            held = held * decay + state[:, k * LANES : (k + 1) * LANES]
        tall = jnp.concatenate([jnp.concatenate(parts, axis=1)] * per, 0)
        own = iota(tall.shape, 0) // modes == (iota(tall.shape, 1) % LANES) // group
        tall = jnp.where(own, tall, 0.0).astype(jnp.bfloat16)
        total = conv[b] + dot(a_high, tall, (1, 0)) + dot(a_low, tall, (1, 0))
        direct = skip[:, lanes]
        for k in range(chunks):
            span = pl.ds(k * SPAN, SPAN)
            value = total[:, k * LANES : (k + 1) * LANES] + direct * prod[b, span, :]
            gath[z, b, span, :] = (query[b, span, :] * value).astype(jnp.bfloat16)

        @pl.when(z > 0)
        def _():
            own_copy(b, z - 1, left_sems).start()

        @pl.when(z < n_tp - 1)
        def _():
            own_copy(b, z + 1, right_sems).start()

        return 0

    def both(b, _):
        filters_of(b + ahead, 0)
        finish(b, 0)
        within(b + ahead, 0)
        return 0

    lax.fori_loop(0, blocks - ahead, both, 0)
    lax.fori_loop(blocks - ahead, blocks, finish, 0)

    def project(shard, p):
        left = jnp.concatenate([gath[shard, 2 * p], gath[shard, 2 * p + 1]], axis=1)
        depth = 2 * LANES
        at = pl.multiple_of(shard * width + p * depth, depth)
        acc[...] += dot(left, w[pl.ds(at, depth), :], (1, 0))

    w_copy.wait()
    acc[...] = jnp.zeros_like(acc)

    def own_step(p, _):
        project(z, p)
        return 0

    def pass_copy(shard, b, to):
        return pltpu.make_async_remote_copy(
            src_ref=gath.at[shard, b],
            dst_ref=gath.at[shard, b],
            send_sem=fwd_sems.at[shard, b],
            recv_sem=recv_sems.at[shard, b],
            device_id=(me, to),
            device_id_type=MESH,
        )

    def hop(i, _):
        d, p = 1 + i // (blocks // 2), i % (blocks // 2)
        above, below = z + d, z - d
        for b in (2 * p, 2 * p + 1):
            @pl.when(above < n_tp)
            def _():
                pass_copy(above, b, lax.rem(z + 1, n_tp)).wait_recv()

                @pl.when(z > 0)
                def _():
                    pass_copy(above, b, z - 1).start()

            @pl.when(below >= 0)
            def _():
                pass_copy(below, b, lax.rem(z + 1, n_tp)).wait_recv()

                @pl.when(z < n_tp - 1)
                def _():
                    pass_copy(below, b, z + 1).start()

        @pl.when(above < n_tp)
        def _():
            project(above, p)

        @pl.when(below >= 0)
        def _():
            project(below, p)

        return 0

    lax.fori_loop(0, blocks // 2, hop, 0)
    lax.fori_loop(0, blocks // 2, own_step, 0)
    lax.fori_loop(blocks // 2, (n_tp - 1) * (blocks // 2), hop, 0)
    out[...] = acc[...].astype(out.dtype)

    @pl.when(me < n_ctx - 1)
    def _():
        halo_copy.wait_send()

    def e_sent(d, _):
        @pl.when(me + d < n_ctx)
        def _():
            e_copy(d).wait_send()

        return 0

    lax.fori_loop(1, n_ctx, e_sent, 0)

    def own_sent(b, _):
        @pl.when(z > 0)
        def _():
            own_copy(b, z - 1, left_sems).wait_send()

        @pl.when(z < n_tp - 1)
        def _():
            own_copy(b, z + 1, right_sems).wait_send()

        return 0

    lax.fori_loop(0, blocks, own_sent, 0)

    def pass_sent(i, _):
        shard, b = i // blocks, i % blocks

        @pl.when((shard > z) & (z > 0))
        def _():
            pass_copy(shard, b, z - 1).wait_send()

        @pl.when((shard < z) & (z < n_tp - 1))
        def _():
            pass_copy(shard, b, z + 1).wait_send()

        return 0

    lax.fori_loop(0, n_tp * blocks, pass_sent, 0)


def shards(n_ctx, n_tp, features, short_taps, residues, rates, skip, out_weight):
    rows, _, width = features.shape
    modes, filters = rates.shape
    group = width // filters
    blocks, chunks = width // LANES, rows // SPAN
    columns = out_weight.shape[1]
    vmem = pl.BlockSpec(memory_space=pltpu.VMEM)
    f32, bf16 = jnp.float32, jnp.bfloat16
    dma = pltpu.SemaphoreType.DMA
    return pl.pallas_call(
        functools.partial(kernel, n_ctx, n_tp, group),
        out_shape=pltpu.VMEM((rows, columns), bf16),
        in_specs=[pl.BlockSpec(memory_space=pl.ANY)] + [vmem] * 4 + [pl.BlockSpec(memory_space=pl.ANY)],
        out_specs=vmem,
        scratch_shapes=[
            pltpu.VMEM((3, rows, width), bf16),
            pltpu.VMEM((3, HALO, width), bf16),
            pltpu.VMEM(out_weight.shape, bf16),
            pltpu.VMEM((n_tp, blocks, rows, LANES), bf16),
            pltpu.VMEM((blocks, rows, LANES), f32),
            pltpu.VMEM((blocks, rows, LANES), f32),
            pltpu.VMEM((blocks, SPAN, chunks * LANES), f32),
            pltpu.VMEM((blocks, SPAN, LANES // group * SPAN), bf16),
            pltpu.VMEM((blocks, modes, chunks * LANES), f32),
            pltpu.VMEM((modes, width), f32),
            pltpu.VMEM((1, width), f32),
            pltpu.VMEM((1, width), f32),
            pltpu.VMEM((modes, width), f32),
            pltpu.VMEM((modes, width), bf16),
            pltpu.VMEM((n_ctx - 1, modes, width), bf16),
            pltpu.VMEM((rows, columns), f32),
            dma(()),
            dma(()),
            dma((2,)),
            dma((n_ctx - 1,)),
            dma((n_ctx - 1,)),
            dma((blocks,)),
            dma((blocks,)),
            dma((n_tp, blocks)),
            dma((n_tp, blocks)),
        ],
        compiler_params=pltpu.CompilerParams(
            collective_id=0, has_side_effects=True, vmem_limit_bytes=63 * 1024 * 1024
        ),
        cost_estimate=pl.CostEstimate(
            flops=2 * rows * width * n_tp * columns,
            bytes_accessed=2 * out_weight.size,
            transcendentals=0,
        ),
    )(
        jnp.transpose(features, (1, 0, 2)), short_taps, residues, rates,
        skip.reshape(1, width), out_weight,
    )


def solution(mesh):
    in_specs = (
        P("ctx", None, "tp"),
        P(None, None, "tp"),
        P(None, "tp"),
        P(None, "tp"),
        P("tp"),
        P(None, "tp"),
    )
    n_ctx, n_tp = mesh.shape["ctx"], mesh.shape["tp"]
    return jax.shard_map(
        functools.partial(shards, n_ctx, n_tp),
        mesh=mesh, in_specs=in_specs, out_specs=P("ctx", "tp"), check_vma=False,
    )
```

```python
import functools

import jax
import jax.numpy as jnp
from jax import lax
from jax.experimental import pallas as pl
from jax.experimental.pallas import tpu as pltpu
from jax.sharding import PartitionSpec as P

MESH = pl.DeviceIdType.MESH
LANES = 128
SPAN = 64
AHEAD = 4
HALO = 16


def iota(shape, dim):
    return lax.broadcasted_iota(jnp.int32, shape, dim)


def split(x):
    high = x.astype(jnp.bfloat16)
    low = (x - high.astype(jnp.float32)).astype(jnp.bfloat16)
    return high, low


def dot(left, right, dims):
    return lax.dot_general(
        left, right, ((dims[:1], dims[1:]), ((), ())), preferred_element_type=jnp.float32
    )


def kernel(
    n_ctx, n_tp, group,
    feats_in, taps, residues, rates, skip, w_hbm, out,
    feats,
    halo, w, gath, prod, query, conv, filts, states, rep_rates, row_rates, row_coefs,
    entering, e_send, e_recv, acc,
    in_sem, w_sem, halo_sems, es_sems, er_sems, left_sems, right_sems, fwd_sems, recv_sems,
):
    me, z = lax.axis_index("ctx"), lax.axis_index("tp")
    rows, width = feats.shape[1], feats.shape[2]
    modes, filters = rates.shape
    blocks, chunks = width // LANES, rows // SPAN
    per = LANES // group

    load = pltpu.make_async_copy(feats_in, feats, in_sem)
    load.start()
    w_copy = pltpu.make_async_copy(w_hbm, w, w_sem)

    barrier = pltpu.get_barrier_semaphore()

    def greet(d, _):
        pl.semaphore_signal(
            barrier, inc=1, device_id=(lax.rem(me + d, n_ctx), z), device_id_type=MESH
        )
        return 0

    lax.fori_loop(1, n_ctx, greet, 0)

    @pl.when(z > 0)
    def _():
        pl.semaphore_signal(barrier, inc=1, device_id=(me, z - 1), device_id_type=MESH)

    @pl.when(z < n_tp - 1)
    def _():
        pl.semaphore_signal(barrier, inc=1, device_id=(me, z + 1), device_id_type=MESH)

    pick = (iota((filters, width), 0) == iota((filters, width), 1) // group).astype(jnp.float32)

    def repeat(x):
        return lax.dot_general(
            x, pick, (((1,), (0,)), ((), ())),
            precision=lax.Precision.HIGHEST, preferred_element_type=jnp.float32,
        )

    diag = iota((modes, width), 0) == iota((modes, width), 1) % modes
    rep_rates[...] = repeat(rates[...])
    row_rates[...] = jnp.sum(jnp.where(diag, rep_rates[...], 0.0), axis=0, keepdims=True)
    row_res = jnp.sum(jnp.where(diag, repeat(residues[...]), 0.0), axis=0, keepdims=True)
    row_coefs[...] = row_res * jnp.sqrt(2.0 * row_rates[...])

    neighbours = (z > 0).astype(jnp.int32) + (z < n_tp - 1).astype(jnp.int32)
    pl.semaphore_wait(barrier, n_ctx - 1 + neighbours)

    halo_copy = pltpu.make_async_remote_copy(
        src_ref=feats_in.at[:, pl.ds(rows - HALO, HALO), :],
        dst_ref=halo,
        send_sem=halo_sems.at[0],
        recv_sem=halo_sems.at[1],
        device_id=(lax.rem(me + 1, n_ctx), z),
        device_id_type=MESH,
    )

    @pl.when(me < n_ctx - 1)
    def _():
        halo_copy.start()

    @pl.when(me == 0)
    def _():
        halo[...] = jnp.zeros_like(halo)

    def lanes_of(b):
        return pl.ds(pl.multiple_of(b * LANES, LANES), LANES)

    def filters_of(b, _):
        lanes = lanes_of(b)
        rate, coef = row_rates[:, lanes], row_coefs[:, lanes]
        at = iota((SPAN, LANES), 0).astype(jnp.float32)
        a_high, a_low = split(coef * jnp.exp(-rate * at))
        rise = jnp.exp(rate * at)
        rise_high = rise.astype(jnp.bfloat16).astype(jnp.float32)
        rise_low = rise - rise_high
        shape = (per * SPAN, LANES)
        own = iota(shape, 0) // SPAN == iota(shape, 1) // modes
        b_high = jnp.where(own, jnp.concatenate([rise_high] * per, 0), 0.0).astype(jnp.bfloat16)
        b_low = jnp.where(own, jnp.concatenate([rise_low] * per, 0), 0.0).astype(jnp.bfloat16)
        filt = (
            dot(a_high, b_high, (1, 1)) + dot(a_low, b_high, (1, 1)) + dot(a_high, b_low, (1, 1))
        )
        filts[b] = jnp.where(
            iota(filt.shape, 0) >= iota(filt.shape, 1) % SPAN, filt, 0.0
        ).astype(jnp.bfloat16)
        return 0

    ahead = min(AHEAD, blocks)
    for b in range(ahead // 2):
        filters_of(b, 0)
    load.wait()
    w_copy.start()

    @pl.when(me > 0)
    def _():
        halo_copy.wait_recv()

    def wide(x):
        return jnp.concatenate([x[k * SPAN : (k + 1) * SPAN] for k in range(chunks)], axis=1)

    def shorted(b, j):
        lanes = lanes_of(b)
        here = feats[j, :, lanes].astype(jnp.float32)
        before = halo[j, :, lanes].astype(jnp.float32)
        row = iota((rows, LANES), 0)
        last, second = before[HALO - 1 : HALO], before[HALO - 2 : HALO - 1]
        one = jnp.where(row == 0, last, pltpu.roll(here, 1, 0))
        two = jnp.where(row == 0, second, jnp.where(row == 1, last, pltpu.roll(here, 2, 0)))
        tap = [taps[s, pl.ds(j, 1), lanes] for s in range(3)]
        return tap[0] * here + tap[1] * one + tap[2] * two

    def first(b, _):
        lanes = lanes_of(b)
        product = shorted(b, 1) * shorted(b, 2)
        prod[b] = product
        rate = row_rates[:, lanes]
        left_over = (SPAN - iota((SPAN, LANES), 0)).astype(jnp.float32)
        high, low = split(jnp.exp(-rate * left_over))
        value = wide(product).astype(jnp.bfloat16)
        full = dot(high, value, (0, 0)) + dot(low, value, (0, 0))
        own = iota(full.shape, 0) // modes == (iota(full.shape, 1) % LANES) // group
        full = jnp.where(own, full, 0.0)
        state = full[:modes]
        for f in range(1, per):
            state = state + full[f * modes : (f + 1) * modes]
        states[b] = state
        decay = jnp.exp(-float(SPAN) * rep_rates[:, lanes])
        total = state[:, :LANES]
        for k in range(1, chunks):
            total = total * decay + state[:, k * LANES : (k + 1) * LANES]
        e_send[:, lanes] = total.astype(jnp.bfloat16)
        return 0

    for b in range(blocks):
        first(b, 0)

    def e_copy(d):
        return pltpu.make_async_remote_copy(
            src_ref=e_send,
            dst_ref=e_recv.at[d - 1],
            send_sem=es_sems.at[d - 1],
            recv_sem=er_sems.at[d - 1],
            device_id=(lax.rem(me + d, n_ctx), z),
            device_id_type=MESH,
        )

    def e_start(d, _):
        @pl.when(me + d < n_ctx)
        def _():
            e_copy(d).start()

        return 0

    lax.fori_loop(1, n_ctx, e_start, 0)

    def within(b, _):
        query[b] = shorted(b, 0)
        value = jnp.concatenate([wide(prod[b])] * per, 0)
        own = iota(value.shape, 0) // SPAN == (iota(value.shape, 1) % LANES) // group
        value = jnp.where(own, value, 0.0).astype(jnp.bfloat16)
        conv[b] = dot(filts[b], value, (1, 0))
        return 0

    for b in range(ahead // 2, ahead):
        filters_of(b, 0)
    for b in range(ahead):
        within(b, 0)

    entering[...] = jnp.zeros_like(entering)

    def e_take(d, _):
        @pl.when(me >= d)
        def _():
            e_copy(d).wait_recv()
            span = ((d - 1) * rows).astype(jnp.float32)
            entering[...] += jnp.exp(-span * rep_rates[...]) * e_recv[d - 1].astype(jnp.float32)

        return 0

    lax.fori_loop(1, n_ctx, e_take, 0)

    def own_copy(b, to, sems):
        return pltpu.make_async_remote_copy(
            src_ref=gath.at[z, b],
            dst_ref=gath.at[z, b],
            send_sem=sems.at[b],
            recv_sem=recv_sems.at[z, b],
            device_id=(me, to),
            device_id_type=MESH,
        )

    def finish(b, _):
        lanes = lanes_of(b)
        rate, coef = row_rates[:, lanes], row_coefs[:, lanes]
        at = iota((SPAN, LANES), 0).astype(jnp.float32)
        a_high, a_low = split(coef * jnp.exp(-rate * at))
        decay = jnp.exp(-float(SPAN) * rep_rates[:, lanes])
        held, parts, state = entering[:, lanes], [], states[b]
        for k in range(chunks):
            parts.append(held)
            held = held * decay + state[:, k * LANES : (k + 1) * LANES]
        tall = jnp.concatenate([jnp.concatenate(parts, axis=1)] * per, 0)
        own = iota(tall.shape, 0) // modes == (iota(tall.shape, 1) % LANES) // group
        tall = jnp.where(own, tall, 0.0).astype(jnp.bfloat16)
        total = conv[b] + dot(a_high, tall, (1, 0)) + dot(a_low, tall, (1, 0))
        direct = skip[:, lanes]
        for k in range(chunks):
            span = pl.ds(k * SPAN, SPAN)
            value = total[:, k * LANES : (k + 1) * LANES] + direct * prod[b, span, :]
            gath[z, b, span, :] = (query[b, span, :] * value).astype(jnp.bfloat16)

        @pl.when(z > 0)
        def _():
            own_copy(b, z - 1, left_sems).start()

        @pl.when(z < n_tp - 1)
        def _():
            own_copy(b, z + 1, right_sems).start()

        return 0

    def both(b, _):
        finish(b, 0)
        filters_of(b + ahead, 0)
        within(b + ahead, 0)
        return 0

    lax.fori_loop(0, blocks - ahead, both, 0)
    lax.fori_loop(blocks - ahead, blocks, finish, 0)

    def project(shard, p):
        left = jnp.concatenate([gath[shard, 2 * p], gath[shard, 2 * p + 1]], axis=1)
        depth = 2 * LANES
        at = pl.multiple_of(shard * width + p * depth, depth)
        acc[...] += dot(left, w[pl.ds(at, depth), :], (1, 0))

    w_copy.wait()
    acc[...] = jnp.zeros_like(acc)

    def own_step(p, _):
        project(z, p)
        return 0

    def pass_copy(shard, b, to):
        return pltpu.make_async_remote_copy(
            src_ref=gath.at[shard, b],
            dst_ref=gath.at[shard, b],
            send_sem=fwd_sems.at[shard, b],
            recv_sem=recv_sems.at[shard, b],
            device_id=(me, to),
            device_id_type=MESH,
        )

    def hop(i, _):
        d, p = 1 + i // (blocks // 2), i % (blocks // 2)
        above, below = z + d, z - d
        for b in (2 * p, 2 * p + 1):
            @pl.when(above < n_tp)
            def _():
                pass_copy(above, b, lax.rem(z + 1, n_tp)).wait_recv()

                @pl.when(z > 0)
                def _():
                    pass_copy(above, b, z - 1).start()

            @pl.when(below >= 0)
            def _():
                pass_copy(below, b, lax.rem(z + 1, n_tp)).wait_recv()

                @pl.when(z < n_tp - 1)
                def _():
                    pass_copy(below, b, z + 1).start()

        @pl.when(above < n_tp)
        def _():
            project(above, p)

        @pl.when(below >= 0)
        def _():
            project(below, p)

        return 0

    lax.fori_loop(0, blocks // 2, hop, 0)
    lax.fori_loop(0, blocks // 2, own_step, 0)
    lax.fori_loop(blocks // 2, (n_tp - 1) * (blocks // 2), hop, 0)
    out[...] = acc[...].astype(out.dtype)

    @pl.when(me < n_ctx - 1)
    def _():
        halo_copy.wait_send()

    def e_sent(d, _):
        @pl.when(me + d < n_ctx)
        def _():
            e_copy(d).wait_send()

        return 0

    lax.fori_loop(1, n_ctx, e_sent, 0)

    def own_sent(b, _):
        @pl.when(z > 0)
        def _():
            own_copy(b, z - 1, left_sems).wait_send()

        @pl.when(z < n_tp - 1)
        def _():
            own_copy(b, z + 1, right_sems).wait_send()

        return 0

    lax.fori_loop(0, blocks, own_sent, 0)

    def pass_sent(i, _):
        shard, b = i // blocks, i % blocks

        @pl.when((shard > z) & (z > 0))
        def _():
            pass_copy(shard, b, z - 1).wait_send()

        @pl.when((shard < z) & (z < n_tp - 1))
        def _():
            pass_copy(shard, b, z + 1).wait_send()

        return 0

    lax.fori_loop(0, n_tp * blocks, pass_sent, 0)


def shards(n_ctx, n_tp, features, short_taps, residues, rates, skip, out_weight):
    rows, _, width = features.shape
    modes, filters = rates.shape
    group = width // filters
    blocks, chunks = width // LANES, rows // SPAN
    columns = out_weight.shape[1]
    vmem = pl.BlockSpec(memory_space=pltpu.VMEM)
    f32, bf16 = jnp.float32, jnp.bfloat16
    dma = pltpu.SemaphoreType.DMA
    return pl.pallas_call(
        functools.partial(kernel, n_ctx, n_tp, group),
        out_shape=pltpu.VMEM((rows, columns), bf16),
        in_specs=[pl.BlockSpec(memory_space=pl.ANY)] + [vmem] * 4 + [pl.BlockSpec(memory_space=pl.ANY)],
        out_specs=vmem,
        scratch_shapes=[
            pltpu.VMEM((3, rows, width), bf16),
            pltpu.VMEM((3, HALO, width), bf16),
            pltpu.VMEM(out_weight.shape, bf16),
            pltpu.VMEM((n_tp, blocks, rows, LANES), bf16),
            pltpu.VMEM((blocks, rows, LANES), f32),
            pltpu.VMEM((blocks, rows, LANES), f32),
            pltpu.VMEM((blocks, SPAN, chunks * LANES), f32),
            pltpu.VMEM((blocks, SPAN, LANES // group * SPAN), bf16),
            pltpu.VMEM((blocks, modes, chunks * LANES), f32),
            pltpu.VMEM((modes, width), f32),
            pltpu.VMEM((1, width), f32),
            pltpu.VMEM((1, width), f32),
            pltpu.VMEM((modes, width), f32),
            pltpu.VMEM((modes, width), bf16),
            pltpu.VMEM((n_ctx - 1, modes, width), bf16),
            pltpu.VMEM((rows, columns), f32),
            dma(()),
            dma(()),
            dma((2,)),
            dma((n_ctx - 1,)),
            dma((n_ctx - 1,)),
            dma((blocks,)),
            dma((blocks,)),
            dma((n_tp, blocks)),
            dma((n_tp, blocks)),
        ],
        compiler_params=pltpu.CompilerParams(
            collective_id=0, has_side_effects=True, vmem_limit_bytes=63 * 1024 * 1024
        ),
        cost_estimate=pl.CostEstimate(
            flops=2 * rows * width * n_tp * columns,
            bytes_accessed=2 * out_weight.size,
            transcendentals=0,
        ),
    )(
        jnp.transpose(features, (1, 0, 2)), short_taps, residues, rates,
        skip.reshape(1, width), out_weight,
    )


def solution(mesh):
    in_specs = (
        P("ctx", None, "tp"),
        P(None, None, "tp"),
        P(None, "tp"),
        P(None, "tp"),
        P("tp"),
        P(None, "tp"),
    )
    n_ctx, n_tp = mesh.shape["ctx"], mesh.shape["tp"]
    return jax.shard_map(
        functools.partial(shards, n_ctx, n_tp),
        mesh=mesh, in_specs=in_specs, out_specs=P("ctx", "tp"), check_vma=False,
    )
```
